256 devices in a mesh: row: 16 (over y, z_hi), col: 16 (over z_lo, x, core).
Axes of the slice: x: 4, y: 4, z: 8 (z_hi: 4, z_lo: 2; z = z_hi * 2 + z_lo), core: 2. Of those that a mesh axis runs over, the one named last changes fastest.
Arguments:
- block_values: float32 [16, 16, 64, 128, 128], P('row', 'col')
- block_slot: int32 [16, 16, 64], P('row', 'col'), may hold values from 0 to 1023, as said below
- block_count: int32 [16, 16], P('row', 'col'), may hold values from 16 to 64, as said below
- probes: float32 [65536, 128], P(('row', 'col'))
Outputs:
- embedding: float32 [65536, 128], P(('row', 'col'))
- velocity: float32 [65536, 128], P(('row', 'col'))
The draws below stay inside these ranges and needn't reach their ends.
Inputs may be any that keep to these rules, and one draw needn't show every extreme that they name: `block_slot`: the 64 positions of one group tile are distinct; a position s stands for local block row s // 32 and local block column s % 32; of the positions with equal (s // 32) // 2 and (s % 32) // 2, at most 1 are among them, and some such group holds 1. The slots k < block_count[r, c] are in use, the others are not part of W; some tile uses all 64 slots.
All inputs are finite; a program needn't handle non-finite values. Where the reference program divides by a largest or mean magnitude, that divisor is 1e-20 or more.
Results may differ from the reference program's by a relative error of at most 0.00024.
Values sent between devices are 32-bit elements; how exact they have to be, the bound alone decides.
No kernel may reach another device: no remote copies, remote signals or barrier semaphores. Data moves between devices by JAX's collectives and lax.ppermute only.
A program may use at most 192 MiB of HBM per device.

```python
import math
import jax
import jax.numpy as jnp
from jax import lax

BLK = 128
P_SIZE = 128
SB = 2
ITERS = 3
KB = 64
ROW_GROUPS = 16
COL_GROUPS = 16
TILE_R = 32
TILE_C = 32
CAP = 1
NBLK = 512
DOCS = 65536


def draw_block_values(key, part):
    key = jax.random.fold_in(key, 5)
    first, second, third = jax.random.split(key, 3)
    block_grid = (ROW_GROUPS, COL_GROUPS, KB, BLK, BLK)
    row_grid = (ROW_GROUPS, COL_GROUPS, KB, BLK, 1)
    spread = jnp.exp(jax.random.uniform(second, row_grid, jnp.float32, math.log(0.3), math.log(3.0)))
    offdiag = jax.random.uniform(first, block_grid, jnp.float32) * spread * (2.0 / BLK)
    diagonal = jax.random.uniform(third, (ROW_GROUPS, COL_GROUPS, KB, BLK), jnp.float32, 1.0, 3.0)
    identity = (jnp.arange(BLK)[:, None] == jnp.arange(BLK)[None, :]).astype(jnp.float32)
    return offdiag + identity * diagonal[..., None]


def draw_block_slot(key, part):
    key = jax.random.fold_in(key, 11)
    first, second = jax.random.split(key)
    slots_total = TILE_R * TILE_C
    regions = ROW_GROUPS * COL_GROUPS
    group_row = jnp.arange(ROW_GROUPS, dtype=jnp.int32)[:, None, None]
    group_column = jnp.arange(COL_GROUPS, dtype=jnp.int32)[None, :, None]
    position = jnp.arange(slots_total, dtype=jnp.int32)[None, None, :]
    local_row = position // TILE_C
    local_column = position % TILE_C
    block_row = group_row * TILE_R + local_row
    block_column = (local_column // SB * COL_GROUPS + group_column) * SB + local_column % SB
    distance = jnp.abs(block_row - block_column)
    region = local_column // SB * COL_GROUPS + local_row // SB
    within = local_row % SB * SB + local_column % SB
    offsets = jax.random.randint(second, (ROW_GROUPS, COL_GROUPS, regions), 0, SB * SB)
    region_full = jnp.broadcast_to(region, (ROW_GROUPS, COL_GROUPS, slots_total)).astype(jnp.int32)
    offset_here = jnp.take_along_axis(offsets, region_full, axis=2)
    eligible = (within - offset_here) % (SB * SB) < CAP
    jitter = jax.random.randint(first, (ROW_GROUPS, COL_GROUPS, slots_total), 0, 4096)
    ranking = jitter + jnp.where(distance <= 2 * SB, 4096, 0) + jnp.where(distance == 0, 8192, 0)
    ranking = ranking + jnp.where(eligible, 16384, 0)
    ranking = ranking * slots_total + (slots_total - 1 - position)
    chosen = lax.top_k(ranking, KB)[1]
    return chosen.astype(jnp.int32)


def draw_block_count(key, part):
    key = jax.random.fold_in(key, 13)
    first, second = jax.random.split(key)
    tiles = ROW_GROUPS * COL_GROUPS
    divisor = 1 + jax.random.randint(first, (tiles,), 0, 4)
    counts = KB // divisor
    chosen_tile = jax.random.randint(second, (), 0, tiles)
    index = jnp.arange(tiles, dtype=jnp.int32)
    counts = jnp.where(index == (chosen_tile + 1) % tiles, KB // 4, counts)
    counts = jnp.where(index == chosen_tile, KB, counts)
    return counts.reshape(ROW_GROUPS, COL_GROUPS).astype(jnp.int32)


def draw_probes(key, part):
    key = jax.random.fold_in(key, 7)
    base_key, row_key, column_key = jax.random.split(key, 3)
    position = jnp.arange(DOCS, dtype=jnp.float32) / max(DOCS - 1, 1)
    row_scale = jnp.exp(jax.random.uniform(row_key, (DOCS,), jnp.float32, 0.0, math.log(10.0)))
    column_scale = jnp.exp(jax.random.uniform(column_key, (P_SIZE,), jnp.float32, 0.0, math.log(10.0)))
    base = jax.random.normal(base_key, (DOCS, P_SIZE), jnp.float32)
    trend = 1.0 + 4.0 * position
    return base * (trend * row_scale)[:, None] * column_scale[None, :] * 0.1


def setup_inputs(seed: int = 0) -> dict:
    splits = jax.random.split(jax.random.key(seed), 5)
    block_values = draw_block_values(jax.random.fold_in(splits[4], 71), 0)
    block_slot = draw_block_slot(jax.random.fold_in(splits[4], 71), 0)
    block_count = draw_block_count(jax.random.fold_in(splits[4], 71), 0)
    probes = draw_probes(jax.random.fold_in(splits[4], 71), 0)
    return {"block_values": block_values, "block_slot": block_slot, "block_count": block_count, "probes": probes}


def block_positions(block_slot):
    group_row = jnp.arange(ROW_GROUPS, dtype=jnp.int32)[:, None, None]
    group_column = jnp.arange(COL_GROUPS, dtype=jnp.int32)[None, :, None]
    local_row = block_slot // TILE_C
    local_column = block_slot % TILE_C
    block_row = group_row * TILE_R + local_row
    block_column = ((local_column // SB) * COL_GROUPS + group_column) * SB + local_column % SB
    return block_row.astype(jnp.int32), block_column.astype(jnp.int32)


def reference(block_values, block_slot, block_count, probes):
    block_row, block_column = block_positions(block_slot)
    in_use = jnp.arange(KB, dtype=jnp.int32)[None, None, :] < block_count[:, :, None]
    flat_shape = (ROW_GROUPS, COL_GROUPS * KB)
    block_row = block_row.reshape(flat_shape)
    block_column = block_column.reshape(flat_shape)
    in_use = in_use.reshape(flat_shape)
    values = block_values.reshape(ROW_GROUPS, COL_GROUPS * KB, BLK, BLK)
    members_all = (values, block_row, block_column, in_use)

    def degree_terms(running, members):
        masked = jnp.where(members[3][:, None, None], members[0], jnp.float32(0))
        running = running + jax.ops.segment_sum(jnp.sum(masked, axis=2), members[1], num_segments=NBLK)
        running = running + jax.ops.segment_sum(jnp.sum(masked, axis=1), members[2], num_segments=NBLK)
        return running, None

    degree = lax.scan(degree_terms, jnp.zeros((NBLK, BLK), jnp.float32), members_all)[0].reshape(DOCS)

    def propagate(current):
        blocks = current.reshape(NBLK, BLK, P_SIZE)

        def accumulate(running, members):
            masked = jnp.where(members[3][:, None, None], members[0], jnp.float32(0))
            forward = jnp.einsum("kab,kbp->kap", masked, blocks[members[2]], precision=lax.Precision.HIGHEST)
            backward = jnp.einsum("kba,kbp->kap", masked, blocks[members[1]], precision=lax.Precision.HIGHEST)
            running = running + jax.ops.segment_sum(forward, members[1], num_segments=NBLK)
            running = running + jax.ops.segment_sum(backward, members[2], num_segments=NBLK)
            return running, None

        return lax.scan(accumulate, jnp.zeros((NBLK, BLK, P_SIZE), jnp.float32), members_all)[0].reshape(DOCS, P_SIZE)

    current = probes
    earlier = probes
    for iteration in range(ITERS):
        averaged = propagate(current) / degree[:, None]
        mean_abs = jnp.sum(jnp.abs(averaged), axis=0) / DOCS
        earlier = current
        current = averaged / mean_abs
    return current, current - earlier
```

```python
import functools

import jax
import jax.numpy as jnp
from jax import lax
from jax.experimental import pallas as pl
from jax.experimental.pallas import tpu as pltpu
from jax.sharding import PartitionSpec as P

BLK = 128
ITERS = 3
VMEM_LIMIT = 40 * 1024 * 1024

ROW_ORDER = [4 * y + z for y, z in (
    (0, 0), (0, 1), (1, 0), (1, 1), (3, 0), (3, 1), (2, 0), (2, 1),
    (0, 3), (0, 2), (3, 3), (3, 2), (1, 3), (1, 2), (2, 3), (2, 2))]
COL_ORDER = [8 * l + 2 * x + c for c in (0, 1) for l, x in (
    (0, 0), (0, 1), (0, 3), (0, 2), (1, 0), (1, 3), (1, 1), (1, 2))]


def swap(x, axis, m):
    return lax.ppermute(x, axis, [(i, i ^ m) for i in range(16)])


def row_swap(x, y=0, z=0):
    return swap(x, "row", 4 * y + z)


def col_swap(x, l=0, x_=0, c=0):
    return swap(x, "col", 8 * l + 2 * x_ + c)


def cat(*parts):
    return jnp.concatenate(parts, axis=0)


def gather_row(x):
    r = row_swap(x, z=1)
    a = cat(x, r)
    b = row_swap(a, z=3)
    a1 = cat(a, row_swap(a, y=1))
    b1 = cat(b, row_swap(b, y=3))
    a2 = row_swap(a1, y=3)
    b2 = row_swap(b1, y=1)
    return [a1, a2, b1, b2]


def gather_col(x):
    b = col_swap(x, l=1)
    a1 = cat(x, col_swap(x, x_=1))
    b1 = cat(b, col_swap(b, x_=3))
    a2 = col_swap(a1, x_=3)
    b2 = col_swap(b1, x_=1)
    return [a1, a2, b1, b2] + [col_swap(p, c=1) for p in (a1, a2, b1, b2)]


def scatter_row(a_keep, a_send, b_keep, b_send):
    a_got = row_swap(a_send, y=3)
    b_got = row_swap(b_send, y=1)
    h = a_keep.shape[0] // 2
    a_got2 = row_swap(a_keep[h:] + a_got[h:], y=1)
    b_got2 = row_swap(b_keep[h:] + b_got[h:], y=3)
    b2 = b_keep[:h] + b_got[:h] + b_got2
    got3 = row_swap(b2, z=3)
    a2 = a_keep[:h] + a_got[:h] + a_got2
    q = h // 2
    got4 = row_swap(a2[q:] + got3[q:], z=1)
    return a2[:q] + got3[:q] + got4


def scatter_col(keep, send):
    got = col_swap(send, c=1)
    q = keep.shape[0] // 4
    part = [keep[i * q:(i + 1) * q] + got[i * q:(i + 1) * q] for i in range(4)]
    a_got = col_swap(part[1], x_=3)
    b_got = col_swap(part[3], x_=1)
    h = q // 2
    a_got2 = col_swap(part[0][h:] + a_got[h:], x_=1)
    b_got2 = col_swap(part[2][h:] + b_got[h:], x_=3)
    got2 = col_swap(part[2][:h] + b_got[:h] + b_got2, l=1)
    return part[0][:h] + a_got[:h] + a_got2 + got2


def global_sum(s):
    for kw in (dict(c=1), dict(x_=1), dict(x_=3), dict(l=1)):
        s = s + col_swap(s, **kw)
    for kw in (dict(z=1), dict(z=3), dict(y=1), dict(y=3)):
        s = s + row_swap(s, **kw)
    return s


def prepare_kernel(row_ref, col_ref, count_ref, w_ref, wh, wl, th, tl, drow, dcol):
    step = pl.program_id(0)

    @pl.when(step == 0)
    def _():
        drow[...] = jnp.zeros_like(drow)
        dcol[...] = jnp.zeros_like(dcol)

    per = w_ref.shape[0]
    for j in range(per):
        k = step * per + j
        w = jnp.where(k < count_ref[0], w_ref[j], 0.0)
        t = w.T
        hi = w.astype(jnp.bfloat16)
        wh[j] = hi
        wl[j] = (w - hi.astype(jnp.float32)).astype(jnp.bfloat16)
        hi = t.astype(jnp.bfloat16)
        th[j] = hi
        tl[j] = (t - hi.astype(jnp.float32)).astype(jnp.bfloat16)
        first = lax.broadcasted_iota(jnp.int32, (8, BLK), 0) == 0
        r, c = row_ref[k], col_ref[k]
        drow[r] += jnp.where(first, jnp.sum(t, axis=0, keepdims=True), 0.0)
        dcol[c] += jnp.where(first, jnp.sum(w, axis=0, keepdims=True), 0.0)


def prepare(values, row_pos, col_pos, count):
    n = values.shape[0]
    per = 8
    nrow, ncol = 32, 32
    blk = pl.BlockSpec((per, BLK, BLK), lambda i, *_: (i, 0, 0))
    deg = pl.BlockSpec((nrow, 8, BLK), lambda i, *_: (0, 0, 0))
    half = jax.ShapeDtypeStruct((n, BLK, BLK), jnp.bfloat16)
    return pl.pallas_call(
        prepare_kernel,
        grid_spec=pltpu.PrefetchScalarGridSpec(
            num_scalar_prefetch=3, grid=(n // per,), in_specs=[blk], out_specs=[blk] * 4 + [deg] * 2
        ),
        out_shape=[half] * 4
        + [jax.ShapeDtypeStruct((nrow, 8, BLK), jnp.float32), jax.ShapeDtypeStruct((ncol, 8, BLK), jnp.float32)],
        compiler_params=pltpu.CompilerParams(vmem_limit_bytes=VMEM_LIMIT),
        name="prepare",
    )(row_pos, col_pos, count, values)


def product_kernel(n_in, n_out, with_deg, src_ref, dst_ref, *refs):
    refs = list(refs)
    wh, wl, inv = refs[:3]
    xs = refs[3:3 + n_in]
    rest = refs[3 + n_in:]
    if with_deg:
        deg, rest = rest[0], rest[1:]
    outs, (xh, xl, acc) = rest[:n_out], rest[n_out:]
    scale = inv[...]
    at = 0
    for x in xs:
        for b in range(x.shape[0] // BLK):
            v = x[b * BLK:(b + 1) * BLK, :] / scale
            hi = v.astype(jnp.bfloat16)
            xh[at] = hi
            xl[at] = (v - hi.astype(jnp.float32)).astype(jnp.bfloat16)
            at += 1
    acc[...] = jnp.zeros_like(acc)
    group = 4

    @pl.loop(0, wh.shape[0] // group)
    def _(g):
        prods = []
        for j in range(group):
            k = g * group + j
            s = src_ref[k]
            a, b, c, d = wh[k], wl[k], xh[s], xl[s]
            p = jnp.dot(a, c, preferred_element_type=jnp.float32)
            p += jnp.dot(b, c, preferred_element_type=jnp.float32)
            p += jnp.dot(a, d, preferred_element_type=jnp.float32)
            prods.append(p)
        for j in range(group):
            d = dst_ref[g * group + j]
            acc[d] += prods[j]

    at = 0
    for o in outs:
        for b in range(o.shape[0]):
            o[b, :BLK, :] = acc[at]
            if with_deg:
                o[b, BLK:, :] = deg[at]
            at += 1


def product(src, dst, wh, wl, mean, xs, sizes, deg=None):
    rows = BLK + (8 if deg is not None else 0)
    smem = pl.BlockSpec(memory_space=pltpu.SMEM)
    vmem = pl.BlockSpec(memory_space=pltpu.VMEM)
    args = [wh, wl, mean, *xs] + ([deg] if deg is not None else [])
    n = wh.shape[0]
    return pl.pallas_call(
        functools.partial(product_kernel, len(xs), len(sizes), deg is not None),
        in_specs=[smem, smem] + [vmem] * len(args),
        out_specs=[vmem] * len(sizes),
        out_shape=[jax.ShapeDtypeStruct((s, rows, BLK), jnp.float32) for s in sizes],
        scratch_shapes=[
            pltpu.VMEM((32, BLK, BLK), jnp.bfloat16),
            pltpu.VMEM((32, BLK, BLK), jnp.bfloat16),
            pltpu.VMEM((32, BLK, BLK), jnp.float32),
        ],
        compiler_params=pltpu.CompilerParams(vmem_limit_bytes=VMEM_LIMIT),
        cost_estimate=pl.CostEstimate(flops=6 * n * BLK**3, bytes_accessed=12 * 2**20, transcendentals=0),
        name="product",
    )(src, dst, *args)


def finish_kernel(r_ref, c_ref, y_ref, d_ref, s_ref):
    total = jnp.zeros((8, BLK), jnp.float32)
    for b in range(2):
        t = r_ref[b] + c_ref[b]
        d = jnp.broadcast_to(t[BLK:BLK + 1, :], (BLK, BLK)).T
        y = t[:BLK] / d
        y_ref[b * BLK:(b + 1) * BLK, :] = y
        d_ref[b * BLK:(b + 1) * BLK, :] = d
        total += jnp.sum(jnp.abs(y).reshape(BLK // 8, 8, BLK), axis=0)
    s_ref[...] = jnp.broadcast_to(jnp.sum(total, axis=0, keepdims=True), (8, BLK))


def finish_first(r, c):
    vmem = pl.BlockSpec(memory_space=pltpu.VMEM)
    big = jax.ShapeDtypeStruct((2 * BLK, BLK), jnp.float32)
    return pl.pallas_call(
        finish_kernel,
        in_specs=[vmem, vmem],
        out_specs=[vmem] * 3,
        out_shape=[big, big, jax.ShapeDtypeStruct((8, BLK), jnp.float32)],
        name="finish",
    )(r, c)


def position(order, index):
    order_pos = [order.index(m) for m in range(16)]
    out = jnp.zeros_like(index)
    for m in range(16):
        out = out + jnp.where(index == m, order_pos[m], 0)
    return out


def local(block_values, block_slot, block_count, probes):
    total_docs = probes.shape[0] * lax.axis_size("row") * lax.axis_size("col")
    slots = block_slot.reshape(-1)
    stored = slots.shape[0]
    local_row, local_col = slots // 32, slots % 32
    row_pos = 2 * position(COL_ORDER, (local_row // 2) ^ lax.axis_index("col")) + local_row % 2
    col_pos = 2 * position(ROW_ORDER, (local_col // 2) ^ lax.axis_index("row")) + local_col % 2
    wh, wl, th, tl, drow, dcol = prepare(
        block_values.reshape(stored, BLK, BLK), row_pos, col_pos, block_count.reshape(1)
    )
    mean = jnp.ones((1, BLK), jnp.float32)
    y = probes
    means = []
    ys = []
    for t in range(ITERS):
        col_parts = gather_col(y)
        row_parts = gather_row(y)
        back = product(row_pos, col_pos, th, tl, mean, col_parts, [8] * 4, dcol if t == 0 else None)
        col_total = scatter_row(*back)
        fwd = product(col_pos, row_pos, wh, wl, mean, row_parts, [16, 16], drow if t == 0 else None)
        row_total = scatter_col(*fwd)
        if t == 0:
            y, deg, part = finish_first(row_total, col_total)
        else:
            y = (row_total + col_total).reshape(2 * BLK, BLK) / deg
            part = jnp.broadcast_to(jnp.sum(jnp.abs(y), axis=0, keepdims=True), (8, BLK))
        mean = global_sum(part)[:1] / total_docs
        means.append(mean)
        ys.append(y)
    current = ys[-1] / means[-1]
    return current, current - ys[-2] / means[-2]


def solution(mesh):
    in_specs = (
        P("row", "col", None, None, None),
        P("row", "col", None),
        P("row", "col"),
        P(("row", "col"), None),
    )
    out_specs = (P(("row", "col"), None), P(("row", "col"), None))
    return jax.shard_map(local, mesh=mesh, in_specs=in_specs, out_specs=out_specs, check_vma=False)
```

```python
import functools

import jax
import jax.numpy as jnp
from jax import lax
from jax.experimental import pallas as pl
from jax.experimental.pallas import tpu as pltpu
from jax.sharding import PartitionSpec as P

BLK = 128
ITERS = 3
VMEM_LIMIT = 40 * 1024 * 1024

ROW_ORDER = [4 * y + z for y, z in (
    (0, 0), (0, 1), (1, 0), (1, 1), (3, 0), (3, 1), (2, 0), (2, 1),
    (0, 3), (0, 2), (3, 3), (3, 2), (1, 3), (1, 2), (2, 3), (2, 2))]
COL_ORDER = [8 * l + 2 * x + c for c in (0, 1) for l, x in (
    (0, 0), (0, 1), (0, 3), (0, 2), (1, 0), (1, 3), (1, 1), (1, 2))]


def swap(x, axis, m):
    return lax.ppermute(x, axis, [(i, i ^ m) for i in range(16)])


def row_swap(x, y=0, z=0):
    return swap(x, "row", 4 * y + z)


def col_swap(x, l=0, x_=0, c=0):
    return swap(x, "col", 8 * l + 2 * x_ + c)


def cat(*parts):
    return jnp.concatenate(parts, axis=0)


def tie(x, *after):
    return lax.optimization_barrier((x, after))[0]


def gather(x, after):
    z1 = row_swap(x, z=1)
    lo = col_swap(x, l=1)
    z3 = row_swap(x, z=3)
    x1 = col_swap(x, x_=1)
    lo3 = col_swap(x, l=1, x_=3)
    z2 = row_swap(x, z=2)
    ra = tie(cat(x, z1), *after)
    ca1 = cat(x, x1)
    cb1 = cat(lo, lo3)
    ry1 = row_swap(ra, y=1)
    rb = tie(cat(z3, z2), ca1, cb1)
    ry3 = row_swap(rb, y=3)
    ca2, cb2 = col_swap(ca1, x_=3), col_swap(cb1, x_=1)
    cols = [ca1, ca2, cb1, cb2]
    cols = cols + [col_swap(p, c=1) for p in cols]
    ra1 = tie(cat(ra, ry1), ca2, cb2)
    ra2 = row_swap(ra1, y=3)
    rb1 = tie(cat(rb, ry3), ca2, cb2)
    rb2 = row_swap(rb1, y=1)
    return [ra1, ra2, rb1, rb2], cols


def weights(refs, scaled):
    if not scaled:
        return [None] * len(refs), None, None
    aux = [r[r.shape[0] - 8:, :] for r in refs]
    scales = [a[:1] for a in aux]
    top = functools.reduce(jnp.maximum, scales)
    return [s / top for s in scales], top, functools.reduce(jnp.add, [a[1:2] for a in aux])


def weighted(refs, starts, weight, i, j):
    total = None
    for r, at, w in zip(refs, starts, weight):
        v = r[at + i:at + j, :]
        v = v if w is None else v * w
        total = v if total is None else total + v
    return total


def aux_tile(scale, total):
    row = lax.broadcasted_iota(jnp.int32, (8, BLK), 0)
    return jnp.where(row == 0, scale, jnp.where(row == 1, total, 0.0))


def mix_kernel(starts, scaled, *refs):
    refs, outs = refs[:len(starts)], refs[len(starts):]
    weight, top, total = weights(refs, scaled)
    at = 0
    for o in outs:
        n = o.shape[0] - (8 if scaled else 0)
        o[:n, :] = weighted(refs, starts, weight, at, at + n)
        if scaled:
            o[n:, :] = aux_tile(top, total)
        at += n


def mix(terms, rows, scaled):
    vmem = pl.BlockSpec(memory_space=pltpu.VMEM)
    tail = 8 if scaled else 0
    return pl.pallas_call(
        functools.partial(mix_kernel, tuple(at for _, at in terms), scaled),
        in_specs=[vmem] * len(terms),
        out_specs=[vmem] * len(rows),
        out_shape=[jax.ShapeDtypeStruct((n + tail, BLK), jnp.float32) for n in rows],
        compiler_params=pltpu.CompilerParams(vmem_limit_bytes=VMEM_LIMIT),
        name="mix",
    )(*[x for x, _ in terms])


def scatter(back, fwd, unit, scaled):
    a_keep, a_send, b_keep, b_send = back
    keep, send = fwd
    a_got, b_got = row_swap(a_send, y=3), row_swap(b_send, y=1)
    send, a_got, b_got = lax.optimization_barrier((send, a_got, b_got))
    got = col_swap(send, c=1)
    two, four = 2 * unit, 4 * unit
    a_got2 = row_swap(mix([(a_keep, four), (a_got, four)], [four], scaled)[0], y=1)
    b_got2 = row_swap(mix([(b_keep, four), (b_got, four)], [four], scaled)[0], y=3)
    ca_got = col_swap(mix([(keep, four), (got, four)], [four], scaled)[0], x_=3)
    cb_got = col_swap(mix([(keep, 3 * four), (got, 3 * four)], [four], scaled)[0], x_=1)
    a_got2, b_got2, ca_got, cb_got = lax.optimization_barrier((a_got2, b_got2, ca_got, cb_got))
    to3, to2 = mix([(b_keep, 0), (b_got, 0), (b_got2, 0)], [two, two], scaled)
    to1, = mix([(a_keep, two), (a_got, two), (a_got2, two)], [two], scaled)
    to_l, to_lx = mix([(keep, 2 * four), (got, 2 * four), (cb_got, 0)], [two, two], scaled)
    to_x, = mix([(keep, two), (got, two), (ca_got, two)], [two], scaled)
    row_terms = [a_keep, a_got, a_got2, row_swap(to1, z=1), row_swap(to2, z=2), row_swap(to3, z=3)]
    col_terms = [keep, got, ca_got, col_swap(to_x, x_=1), col_swap(to_l, l=1), col_swap(to_lx, l=1, x_=3)]
    return row_terms, col_terms


def row_sum(s):
    for kw in (dict(z=1), dict(z=3), dict(y=1), dict(y=3)):
        s = s + row_swap(s, **kw)
    return s


def prepare_kernel(row_ref, col_ref, count_ref, w_ref, wh, wl, th, tl, drow, dcol):
    step = pl.program_id(0)

    @pl.when(step == 0)
    def _():
        drow[...] = jnp.zeros_like(drow)
        dcol[...] = jnp.zeros_like(dcol)

    per = w_ref.shape[0]
    for j in range(per):
        k = step * per + j
        w = jnp.where(k < count_ref[0], w_ref[j], 0.0)
        t = w.T
        hi = w.astype(jnp.bfloat16)
        wh[j] = hi
        wl[j] = (w - hi.astype(jnp.float32)).astype(jnp.bfloat16)
        hi = t.astype(jnp.bfloat16)
        th[j] = hi
        tl[j] = (t - hi.astype(jnp.float32)).astype(jnp.bfloat16)
        first = lax.broadcasted_iota(jnp.int32, (8, BLK), 0) == 0
        r, c = row_ref[k], col_ref[k]
        drow[r] += jnp.where(first, jnp.sum(t, axis=0, keepdims=True), 0.0)
        dcol[c] += jnp.where(first, jnp.sum(w, axis=0, keepdims=True), 0.0)


def prepare(values, row_pos, col_pos, count):
    n = values.shape[0]
    per = 8
    nrow, ncol = 32, 32
    blk = pl.BlockSpec((per, BLK, BLK), lambda i, *_: (i, 0, 0))
    deg = pl.BlockSpec((nrow, 8, BLK), lambda i, *_: (0, 0, 0))
    half = jax.ShapeDtypeStruct((n, BLK, BLK), jnp.bfloat16)
    return pl.pallas_call(
        prepare_kernel,
        grid_spec=pltpu.PrefetchScalarGridSpec(
            num_scalar_prefetch=3, grid=(n // per,), in_specs=[blk], out_specs=[blk] * 4 + [deg] * 2
        ),
        out_shape=[half] * 4
        + [jax.ShapeDtypeStruct((nrow, 8, BLK), jnp.float32), jax.ShapeDtypeStruct((ncol, 8, BLK), jnp.float32)],
        compiler_params=pltpu.CompilerParams(vmem_limit_bytes=VMEM_LIMIT),
        name="prepare",
    )(row_pos, col_pos, count, values)


def product_kernel(n_in, unit, src_ref, dst_ref, *refs):
    refs = list(refs)
    wh, wl = refs[:2]
    xs = refs[2:2 + n_in]
    rest = refs[2 + n_in:]
    if unit > BLK:
        deg, rest = rest[0], rest[1:]
    outs, (xh, xl, acc) = rest[:-3], rest[-3:]
    if unit == BLK:
        top = jnp.zeros((8, BLK), jnp.float32)
        total = jnp.zeros((8, BLK), jnp.float32)
        for x in xs:
            size = jnp.abs(x[...]).reshape(-1, 8, BLK)
            top = jnp.maximum(top, jnp.max(size, axis=0))
            total += jnp.sum(size, axis=0)
        total = jnp.sum(total, axis=0, keepdims=True)
        top = jnp.max(top, axis=0, keepdims=True)
        scale = jnp.where(top > 1e-30, top, 1e-30)
    at = 0
    for x in xs:
        for b in range(x.shape[0] // BLK):
            v = x[b * BLK:(b + 1) * BLK, :]
            if unit == BLK:
                v = v / scale
            hi = v.astype(jnp.bfloat16)
            xh[at] = hi
            xl[at] = (v - hi.astype(jnp.float32)).astype(jnp.bfloat16)
            at += 1
    acc[...] = jnp.zeros_like(acc)
    group = 4

    @pl.loop(0, wh.shape[0] // group)
    def _(g):
        prods = []
        for j in range(group):
            k = g * group + j
            s = src_ref[k]
            a, b, c, d = wh[k], wl[k], xh[s], xl[s]
            p = jnp.dot(a, c, preferred_element_type=jnp.float32)
            p += jnp.dot(b, c, preferred_element_type=jnp.float32)
            p += jnp.dot(a, d, preferred_element_type=jnp.float32)
            prods.append(p)
        for j in range(group):
            d = dst_ref[g * group + j]
            acc[d] += prods[j]

    at = 0
    for o in outs:
        for b in range(o.shape[0] // unit):
            o[b * unit:b * unit + BLK, :] = acc[at]
            if unit > BLK:
                o[b * unit + BLK:(b + 1) * unit, :] = deg[at]
            at += 1
        if unit == BLK:
            o[o.shape[0] - 8:, :] = aux_tile(scale, total)


def product(src, dst, wh, wl, xs, sizes, deg=None):
    unit, tail = (BLK, 8) if deg is None else (BLK + 8, 0)
    smem = pl.BlockSpec(memory_space=pltpu.SMEM)
    vmem = pl.BlockSpec(memory_space=pltpu.VMEM)
    args = [wh, wl, *xs] + ([deg] if deg is not None else [])
    n = wh.shape[0]
    return pl.pallas_call(
        functools.partial(product_kernel, len(xs), unit),
        in_specs=[smem, smem] + [vmem] * len(args),
        out_specs=[vmem] * len(sizes),
        out_shape=[jax.ShapeDtypeStruct((s * unit + tail, BLK), jnp.float32) for s in sizes],
        scratch_shapes=[
            pltpu.VMEM((32, BLK, BLK), jnp.bfloat16),
            pltpu.VMEM((32, BLK, BLK), jnp.bfloat16),
            pltpu.VMEM((32, BLK, BLK), jnp.float32),
        ],
        compiler_params=pltpu.CompilerParams(vmem_limit_bytes=VMEM_LIMIT),
        cost_estimate=pl.CostEstimate(flops=6 * n * BLK**3, bytes_accessed=12 * 2**20, transcendentals=0),
        name="product",
    )(src, dst, *args)


def finish_first_kernel(*refs):
    terms, (y_ref, d_ref) = refs[:-2], refs[-2:]
    u = BLK + 8
    for b in range(2):
        t = weighted(terms, [0] * len(terms), [None] * len(terms), b * u, (b + 1) * u)
        d = jnp.broadcast_to(t[BLK:BLK + 1, :], (BLK, BLK)).T
        y_ref[b * BLK:(b + 1) * BLK, :] = t[:BLK] / d
        d_ref[b * BLK:(b + 1) * BLK, :] = d


def finish_kernel(docs, n_row, *refs):
    terms, (d_ref, y_ref, m_ref) = refs[:-3], refs[-3:]
    aux = [r[r.shape[0] - 8:, :] for r in terms]
    mean = functools.reduce(jnp.add, [a[1:2] for a in aux[:n_row]]) / docs
    weight = [a[:1] / mean for a in aux]
    y_ref[...] = weighted(terms, [0] * len(terms), weight, 0, 2 * BLK) / d_ref[...]
    m_ref[...] = jnp.broadcast_to(mean, (8, BLK))


def finish(row_terms, col_terms, deg, docs):
    vmem = pl.BlockSpec(memory_space=pltpu.VMEM)
    big = jax.ShapeDtypeStruct((2 * BLK, BLK), jnp.float32)
    if deg is None:
        kernel, extra, small = finish_first_kernel, [], big
    else:
        kernel, extra = functools.partial(finish_kernel, float(docs), len(row_terms)), [deg]
        small = jax.ShapeDtypeStruct((8, BLK), jnp.float32)
    args = [*row_terms, *col_terms, *extra]
    return pl.pallas_call(
        kernel,
        in_specs=[vmem] * len(args),
        out_specs=[vmem] * 2,
        out_shape=[big, small],
        compiler_params=pltpu.CompilerParams(vmem_limit_bytes=VMEM_LIMIT),
        name="finish",
    )(*args)


def position(order, index):
    order_pos = [order.index(m) for m in range(16)]
    out = jnp.zeros_like(index)
    for m in range(16):
        out = out + jnp.where(index == m, order_pos[m], 0)
    return out


def local(block_values, block_slot, block_count, probes):
    total_docs = probes.shape[0] * lax.axis_size("row") * lax.axis_size("col")
    slots = block_slot.reshape(-1)
    stored = slots.shape[0]
    local_row, local_col = slots // 32, slots % 32
    row_pos = 2 * position(COL_ORDER, (local_row // 2) ^ lax.axis_index("col")) + local_row % 2
    col_pos = 2 * position(ROW_ORDER, (local_col // 2) ^ lax.axis_index("row")) + local_col % 2
    wh, wl, th, tl, drow, dcol = prepare(
        block_values.reshape(stored, BLK, BLK), row_pos, col_pos, block_count.reshape(1)
    )
    y, deg, mean = probes, None, None
    for t in range(ITERS):
        first = t == 0
        before = y
        rows, cols = gather(y, (wh,) if first else ())
        back = product(row_pos, col_pos, th, tl, cols, [8] * 4, dcol if first else None)
        fwd = product(col_pos, row_pos, wh, wl, rows, [16, 16], drow if first else None)
        terms = scatter(back, fwd, BLK + (8 if first else 0), not first)
        if first:
            y, deg = finish(*terms, None, total_docs)
        else:
            y, mean = finish(*terms, deg, total_docs)
    part = jnp.sum(jnp.abs(y).reshape(-1, 8, BLK), axis=0)
    part = jnp.sum(lax.all_to_all(jnp.broadcast_to(part, (16, 8, BLK)), "col", 0, 0, tiled=True), axis=0)
    final = jnp.sum(row_sum(part), axis=0, keepdims=True) / total_docs
    embedding = y / final
    return embedding, embedding - before / mean[:1]


def solution(mesh):
    in_specs = (
        P("row", "col", None, None, None),
        P("row", "col", None),
        P("row", "col"),
        P(("row", "col"), None),
    )
    out_specs = (P(("row", "col"), None), P(("row", "col"), None))
    return jax.shard_map(local, mesh=mesh, in_specs=in_specs, out_specs=out_specs, check_vma=False)
```

```python
import functools

import jax
import jax.numpy as jnp
from jax import lax
from jax.experimental import pallas as pl
from jax.experimental.pallas import tpu as pltpu
from jax.sharding import PartitionSpec as P

BLK = 128
ITERS = 3
VMEM_LIMIT = 40 * 1024 * 1024

ROW_ORDER = [4 * y + z for y, z in (
    (0, 0), (0, 1), (1, 0), (1, 1), (3, 0), (3, 1), (2, 0), (2, 1),
    (0, 3), (0, 2), (3, 3), (3, 2), (1, 3), (1, 2), (2, 3), (2, 2))]
COL_ORDER = [8 * l + 2 * x + c for c in (0, 1) for l, x in (
    (0, 0), (0, 1), (0, 3), (0, 2), (1, 0), (1, 3), (1, 1), (1, 2))]


def swap(x, axis, m):
    return lax.ppermute(x, axis, [(i, i ^ m) for i in range(16)])


def row_swap(x, y=0, z=0):
    return swap(x, "row", 4 * y + z)


def col_swap(x, l=0, x_=0, c=0):
    return swap(x, "col", 8 * l + 2 * x_ + c)


def cat(*parts):
    return jnp.concatenate(parts, axis=0)


def tie(x, *after):
    return lax.optimization_barrier((x, after))[0]


def gather(x, after):
    z1 = row_swap(x, z=1)
    lo = col_swap(x, l=1)
    z3 = row_swap(x, z=3)
    x1 = col_swap(x, x_=1)
    lo3 = col_swap(x, l=1, x_=3)
    z2 = row_swap(x, z=2)
    ra = cat(x, z1)
    ca1 = cat(x, x1)
    cb1 = cat(lo, lo3)
    ry1 = row_swap(ra, y=1)
    rb = tie(cat(z3, z2), ry1, ca1, cb1, *after)
    ry3 = row_swap(rb, y=3)
    ca2, cb2 = col_swap(ca1, x_=3), col_swap(cb1, x_=1)
    cols = [ca1, ca2, cb1, cb2]
    cols = cols + [col_swap(p, c=1) for p in cols]
    ra1 = cat(ra, ry1)
    ra2 = row_swap(ra1, y=3)
    rb1 = tie(cat(rb, ry3), ca2, cb2)
    rb2 = row_swap(rb1, y=1)
    return [ra1, ra2, rb1, rb2], cols


def weights(refs, scaled):
    if not scaled:
        return [None] * len(refs), None, None
    aux = [r[r.shape[0] - 8:, :] for r in refs]
    scales = [a[:1] for a in aux]
    top = functools.reduce(jnp.maximum, scales)
    return [s / top for s in scales], top, functools.reduce(jnp.add, [a[1:2] for a in aux])


def weighted(refs, starts, weight, i, j):
    total = None
    for r, at, w in zip(refs, starts, weight):
        v = r[at + i:at + j, :]
        v = v if w is None else v * w
        total = v if total is None else total + v
    return total


def aux_tile(scale, total):
    row = lax.broadcasted_iota(jnp.int32, (8, BLK), 0)
    return jnp.where(row == 0, scale, jnp.where(row == 1, total, 0.0))


def mix_kernel(starts, scaled, *refs):
    refs, outs = refs[:len(starts)], refs[len(starts):]
    weight, top, total = weights(refs, scaled)
    at = 0
    for o in outs:
        n = o.shape[0] - (8 if scaled else 0)
        o[:n, :] = weighted(refs, starts, weight, at, at + n)
        if scaled:
            o[n:, :] = aux_tile(top, total)
        at += n


def mix(terms, rows, scaled):
    vmem = pl.BlockSpec(memory_space=pltpu.VMEM)
    tail = 8 if scaled else 0
    return pl.pallas_call(
        functools.partial(mix_kernel, tuple(at for _, at in terms), scaled),
        in_specs=[vmem] * len(terms),
        out_specs=[vmem] * len(rows),
        out_shape=[jax.ShapeDtypeStruct((n + tail, BLK), jnp.float32) for n in rows],
        compiler_params=pltpu.CompilerParams(vmem_limit_bytes=VMEM_LIMIT),
        name="mix",
    )(*[x for x, _ in terms])


def scatter(back, fwd, unit, scaled):
    a_keep, a_send, b_keep, b_send = back
    keep, send = fwd
    a_got, b_got = row_swap(a_send, y=3), row_swap(b_send, y=1)
    send, a_got, b_got = lax.optimization_barrier((send, a_got, b_got))
    got = col_swap(send, c=1)
    two, four = 2 * unit, 4 * unit
    a_got2 = row_swap(mix([(a_keep, four), (a_got, four)], [four], scaled)[0], y=1)
    b_got2 = row_swap(mix([(b_keep, four), (b_got, four)], [four], scaled)[0], y=3)
    ca_got = col_swap(mix([(keep, four), (got, four)], [four], scaled)[0], x_=3)
    cb_got = col_swap(mix([(keep, 3 * four), (got, 3 * four)], [four], scaled)[0], x_=1)
    a_got2, b_got2, ca_got, cb_got = lax.optimization_barrier((a_got2, b_got2, ca_got, cb_got))
    to3, to2 = mix([(b_keep, 0), (b_got, 0), (b_got2, 0)], [two, two], scaled)
    to1, = mix([(a_keep, two), (a_got, two), (a_got2, two)], [two], scaled)
    to_l, to_lx = mix([(keep, 2 * four), (got, 2 * four), (cb_got, 0)], [two, two], scaled)
    to_x, = mix([(keep, two), (got, two), (ca_got, two)], [two], scaled)
    row_terms = [a_keep, a_got, a_got2, row_swap(to1, z=1), row_swap(to2, z=2), row_swap(to3, z=3)]
    row_terms = mix([(x, 0) for x in row_terms], [two], scaled)
    col_terms = [keep, got, ca_got, col_swap(to_x, x_=1), col_swap(to_l, l=1), col_swap(to_lx, l=1, x_=3)]
    return row_terms, col_terms


def row_sum(s):
    for kw in (dict(z=1), dict(z=3), dict(y=1), dict(y=3)):
        s = s + row_swap(s, **kw)
    return s


def prepare_kernel(row_ref, col_ref, count_ref, w_ref, wh, wl, th, tl, drow, dcol):
    step = pl.program_id(0)

    @pl.when(step == 0)
    def _():
        drow[...] = jnp.zeros_like(drow)
        dcol[...] = jnp.zeros_like(dcol)

    per = w_ref.shape[0]
    for j in range(per):
        k = step * per + j
        w = jnp.where(k < count_ref[0], w_ref[j], 0.0)
        t = w.T
        hi = w.astype(jnp.bfloat16)
        wh[j] = hi
        wl[j] = (w - hi.astype(jnp.float32)).astype(jnp.bfloat16)
        hi = t.astype(jnp.bfloat16)
        th[j] = hi
        tl[j] = (t - hi.astype(jnp.float32)).astype(jnp.bfloat16)
        first = lax.broadcasted_iota(jnp.int32, (8, BLK), 0) == 0
        r, c = row_ref[k], col_ref[k]
        drow[r] += jnp.where(first, jnp.sum(t, axis=0, keepdims=True), 0.0)
        dcol[c] += jnp.where(first, jnp.sum(w, axis=0, keepdims=True), 0.0)


def prepare(values, row_pos, col_pos, count):
    n = values.shape[0]
    per = 8
    nrow, ncol = 32, 32
    blk = pl.BlockSpec((per, BLK, BLK), lambda i, *_: (i, 0, 0))
    deg = pl.BlockSpec((nrow, 8, BLK), lambda i, *_: (0, 0, 0))
    half = jax.ShapeDtypeStruct((n, BLK, BLK), jnp.bfloat16)
    return pl.pallas_call(
        prepare_kernel,
        grid_spec=pltpu.PrefetchScalarGridSpec(
            num_scalar_prefetch=3, grid=(n // per,), in_specs=[blk], out_specs=[blk] * 4 + [deg] * 2
        ),
        out_shape=[half] * 4
        + [jax.ShapeDtypeStruct((nrow, 8, BLK), jnp.float32), jax.ShapeDtypeStruct((ncol, 8, BLK), jnp.float32)],
        compiler_params=pltpu.CompilerParams(vmem_limit_bytes=VMEM_LIMIT),
        name="prepare",
    )(row_pos, col_pos, count, values)


def product_kernel(n_in, unit, src_ref, dst_ref, *refs):
    refs = list(refs)
    wh, wl = refs[:2]
    xs = refs[2:2 + n_in]
    rest = refs[2 + n_in:]
    if unit > BLK:
        deg, rest = rest[0], rest[1:]
    outs, (xh, xl, acc) = rest[:-3], rest[-3:]
    if unit == BLK:
        top = jnp.zeros((8, BLK), jnp.float32)
        total = jnp.zeros((8, BLK), jnp.float32)
        for x in xs:
            size = jnp.abs(x[...]).reshape(-1, 8, BLK)
            top = jnp.maximum(top, jnp.max(size, axis=0))
            total += jnp.sum(size, axis=0)
        total = jnp.sum(total, axis=0, keepdims=True)
        top = jnp.max(top, axis=0, keepdims=True)
        scale = jnp.where(top > 1e-30, top, 1e-30)
    at = 0
    for x in xs:
        for b in range(x.shape[0] // BLK):
            v = x[b * BLK:(b + 1) * BLK, :]
            if unit == BLK:
                v = v / scale
            hi = v.astype(jnp.bfloat16)
            xh[at] = hi
            xl[at] = (v - hi.astype(jnp.float32)).astype(jnp.bfloat16)
            at += 1
    acc[...] = jnp.zeros_like(acc)
    group = 4

    @pl.loop(0, wh.shape[0] // group)
    def _(g):
        prods = []
        for j in range(group):
            k = g * group + j
            s = src_ref[k]
            a, b, c, d = wh[k], wl[k], xh[s], xl[s]
            p = jnp.dot(a, c, preferred_element_type=jnp.float32)
            p += jnp.dot(b, c, preferred_element_type=jnp.float32)
            p += jnp.dot(a, d, preferred_element_type=jnp.float32)
            prods.append(p)
        for j in range(group):
            d = dst_ref[g * group + j]
            acc[d] += prods[j]

    at = 0
    for o in outs:
        for b in range(o.shape[0] // unit):
            o[b * unit:b * unit + BLK, :] = acc[at]
            if unit > BLK:
                o[b * unit + BLK:(b + 1) * unit, :] = deg[at]
            at += 1
        if unit == BLK:
            o[o.shape[0] - 8:, :] = aux_tile(scale, total)


def product(src, dst, wh, wl, xs, sizes, deg=None):
    unit, tail = (BLK, 8) if deg is None else (BLK + 8, 0)
    smem = pl.BlockSpec(memory_space=pltpu.SMEM)
    vmem = pl.BlockSpec(memory_space=pltpu.VMEM)
    args = [wh, wl, *xs] + ([deg] if deg is not None else [])
    n = wh.shape[0]
    return pl.pallas_call(
        functools.partial(product_kernel, len(xs), unit),
        in_specs=[smem, smem] + [vmem] * len(args),
        out_specs=[vmem] * len(sizes),
        out_shape=[jax.ShapeDtypeStruct((s * unit + tail, BLK), jnp.float32) for s in sizes],
        scratch_shapes=[
            pltpu.VMEM((32, BLK, BLK), jnp.bfloat16),
            pltpu.VMEM((32, BLK, BLK), jnp.bfloat16),
            pltpu.VMEM((32, BLK, BLK), jnp.float32),
        ],
        compiler_params=pltpu.CompilerParams(vmem_limit_bytes=VMEM_LIMIT),
        cost_estimate=pl.CostEstimate(flops=6 * n * BLK**3, bytes_accessed=12 * 2**20, transcendentals=0),
        name="product",
    )(src, dst, *args)


def finish_first_kernel(*refs):
    terms, (y_ref, d_ref) = refs[:-2], refs[-2:]
    u = BLK + 8
    for b in range(2):
        t = weighted(terms, [0] * len(terms), [None] * len(terms), b * u, (b + 1) * u)
        d = jnp.broadcast_to(t[BLK:BLK + 1, :], (BLK, BLK)).T
        y_ref[b * BLK:(b + 1) * BLK, :] = t[:BLK] / d
        d_ref[b * BLK:(b + 1) * BLK, :] = d


def finish_kernel(docs, n_row, *refs):
    terms, (d_ref, y_ref, m_ref) = refs[:-3], refs[-3:]
    aux = [r[r.shape[0] - 8:, :] for r in terms]
    mean = functools.reduce(jnp.add, [a[1:2] for a in aux[:n_row]]) / docs
    weight = [a[:1] / mean for a in aux]
    y_ref[...] = weighted(terms, [0] * len(terms), weight, 0, 2 * BLK) / d_ref[...]
    m_ref[...] = jnp.broadcast_to(mean, (8, BLK))


def finish(row_terms, col_terms, deg, docs):
    vmem = pl.BlockSpec(memory_space=pltpu.VMEM)
    big = jax.ShapeDtypeStruct((2 * BLK, BLK), jnp.float32)
    if deg is None:
        kernel, extra, small = finish_first_kernel, [], big
    else:
        kernel, extra = functools.partial(finish_kernel, float(docs), len(row_terms)), [deg]
        small = jax.ShapeDtypeStruct((8, BLK), jnp.float32)
    args = [*row_terms, *col_terms, *extra]
    return pl.pallas_call(
        kernel,
        in_specs=[vmem] * len(args),
        out_specs=[vmem] * 2,
        out_shape=[big, small],
        compiler_params=pltpu.CompilerParams(vmem_limit_bytes=VMEM_LIMIT),
        name="finish",
    )(*args)


def position(order, index):
    order_pos = [order.index(m) for m in range(16)]
    out = jnp.zeros_like(index)
    for m in range(16):
        out = out + jnp.where(index == m, order_pos[m], 0)
    return out


def local(block_values, block_slot, block_count, probes):
    total_docs = probes.shape[0] * lax.axis_size("row") * lax.axis_size("col")
    slots = block_slot.reshape(-1)
    stored = slots.shape[0]
    local_row, local_col = slots // 32, slots % 32
    row_pos = 2 * position(COL_ORDER, (local_row // 2) ^ lax.axis_index("col")) + local_row % 2
    col_pos = 2 * position(ROW_ORDER, (local_col // 2) ^ lax.axis_index("row")) + local_col % 2
    wh, wl, th, tl, drow, dcol = prepare(
        block_values.reshape(stored, BLK, BLK), row_pos, col_pos, block_count.reshape(1)
    )
    y, deg, mean = probes, None, None
    for t in range(ITERS):
        first = t == 0
        before = y
        rows, cols = gather(y, (wh,) if first else ())
        back = product(row_pos, col_pos, th, tl, cols, [8] * 4, dcol if first else None)
        fwd = product(col_pos, row_pos, wh, wl, rows, [16, 16], drow if first else None)
        terms = scatter(back, fwd, BLK + (8 if first else 0), not first)
        if first:
            y, deg = finish(*terms, None, total_docs)
        else:
            y, mean = finish(*terms, deg, total_docs)
    part = jnp.sum(jnp.abs(y).reshape(-1, 8, BLK), axis=0)
    part = jnp.sum(lax.all_to_all(jnp.broadcast_to(part, (16, 8, BLK)), "col", 0, 0, tiled=True), axis=0)
    final = jnp.sum(row_sum(part), axis=0, keepdims=True) / total_docs
    embedding = y / final
    return embedding, embedding - before / mean[:1]


def solution(mesh):
    in_specs = (
        P("row", "col", None, None, None),
        P("row", "col", None),
        P("row", "col"),
        P(("row", "col"), None),
    )
    out_specs = (P(("row", "col"), None), P(("row", "col"), None))
    return jax.shard_map(local, mesh=mesh, in_specs=in_specs, out_specs=out_specs, check_vma=False)
```

```python
import functools

import jax
import jax.numpy as jnp
from jax import lax
from jax.experimental import pallas as pl
from jax.experimental.pallas import tpu as pltpu
from jax.sharding import PartitionSpec as P

BLK = 128
ITERS = 3
VMEM_LIMIT = 40 * 1024 * 1024

ROW_ORDER = [4 * y + z for y, z in (
    (0, 0), (0, 1), (1, 0), (1, 1), (3, 0), (3, 1), (2, 0), (2, 1),
    (0, 3), (0, 2), (3, 3), (3, 2), (1, 3), (1, 2), (2, 3), (2, 2))]
COL_ORDER = [8 * l + 2 * x + c for c in (0, 1) for l, x in (
    (0, 0), (0, 1), (0, 3), (0, 2), (1, 0), (1, 3), (1, 1), (1, 2))]


def swap(x, axis, m):
    return lax.ppermute(x, axis, [(i, i ^ m) for i in range(16)])


def row_swap(x, y=0, z=0):
    return swap(x, "row", 4 * y + z)


def col_swap(x, l=0, x_=0, c=0):
    return swap(x, "col", 8 * l + 2 * x_ + c)


def cat(*parts):
    return jnp.concatenate(parts, axis=0)


def tie(x, *after):
    return lax.optimization_barrier((x, after))[0]


def gather(x, after):
    z1 = row_swap(x, z=1)
    lo = col_swap(x, l=1)
    z3 = row_swap(x, z=3)
    x1 = col_swap(x, x_=1)
    lo3 = col_swap(x, l=1, x_=3)
    z2 = row_swap(x, z=2)
    ra = cat(x, z1)
    ca1 = cat(x, x1)
    cb1 = cat(lo, lo3)
    ry1 = row_swap(ra, y=1)
    rb = tie(cat(z3, z2), ry1, ca1, cb1, *after)
    ry3 = row_swap(rb, y=3)
    ca2, cb2 = col_swap(ca1, x_=3), col_swap(cb1, x_=1)
    cols = [ca1, ca2, cb1, cb2]
    cols = cols + [col_swap(p, c=1) for p in cols]
    ra1 = cat(ra, ry1)
    ra2 = row_swap(ra1, y=3)
    rb1 = tie(cat(rb, ry3), ca2, cb2)
    rb2 = row_swap(rb1, y=1)
    return [ra1, ra2, rb1, rb2], cols


def weights(refs, scaled):
    if not scaled:
        return [None] * len(refs), None, None
    aux = [r[r.shape[0] - 8:, :] for r in refs]
    scales = [a[:1] for a in aux]
    top = functools.reduce(jnp.maximum, scales)
    return [s / top for s in scales], top, functools.reduce(jnp.add, [a[1:2] for a in aux])


def weighted(refs, starts, weight, i, j):
    total = None
    for r, at, w in zip(refs, starts, weight):
        v = r[at + i:at + j, :]
        v = v if w is None else v * w
        total = v if total is None else total + v
    return total


def aux_tile(scale, total):
    row = lax.broadcasted_iota(jnp.int32, (8, BLK), 0)
    return jnp.where(row == 0, scale, jnp.where(row == 1, total, 0.0))


def mix_kernel(starts, scaled, *refs):
    refs, outs = refs[:len(starts)], refs[len(starts):]
    weight, top, total = weights(refs, scaled)
    at = 0
    for o in outs:
        n = o.shape[0] - (8 if scaled else 0)
        o[:n, :] = weighted(refs, starts, weight, at, at + n)
        if scaled:
            o[n:, :] = aux_tile(top, total)
        at += n


def mix(terms, rows, scaled):
    vmem = pl.BlockSpec(memory_space=pltpu.VMEM)
    tail = 8 if scaled else 0
    return pl.pallas_call(
        functools.partial(mix_kernel, tuple(at for _, at in terms), scaled),
        in_specs=[vmem] * len(terms),
        out_specs=[vmem] * len(rows),
        out_shape=[jax.ShapeDtypeStruct((n + tail, BLK), jnp.float32) for n in rows],
        compiler_params=pltpu.CompilerParams(vmem_limit_bytes=VMEM_LIMIT),
        name="mix",
    )(*[x for x, _ in terms])


def scatter(back, fwd, unit, scaled):
    a_keep, a_send, b_keep, b_send = back
    keep, send = fwd
    a_got, b_got = row_swap(a_send, y=3), row_swap(b_send, y=1)
    send, a_got, b_got = lax.optimization_barrier((send, a_got, b_got))
    got = col_swap(send, c=1)
    two, four = 2 * unit, 4 * unit
    a_got2 = row_swap(mix([(a_keep, four), (a_got, four)], [four], scaled)[0], y=1)
    b_got2 = row_swap(mix([(b_keep, four), (b_got, four)], [four], scaled)[0], y=3)
    ca_got = col_swap(mix([(keep, four), (got, four)], [four], scaled)[0], x_=3)
    cb_got = col_swap(mix([(keep, 3 * four), (got, 3 * four)], [four], scaled)[0], x_=1)
    a_got2, b_got2, ca_got, cb_got = lax.optimization_barrier((a_got2, b_got2, ca_got, cb_got))
    to3, to2 = mix([(b_keep, 0), (b_got, 0), (b_got2, 0)], [two, two], scaled)
    to1, = mix([(a_keep, two), (a_got, two), (a_got2, two)], [two], scaled)
    to_l, to_lx = mix([(keep, 2 * four), (got, 2 * four), (cb_got, 0)], [two, two], scaled)
    to_x, = mix([(keep, two), (got, two), (ca_got, two)], [two], scaled)
    row_terms = [a_keep, a_got, a_got2, row_swap(to1, z=1), row_swap(to2, z=2), row_swap(to3, z=3)]
    row_terms = mix([(x, 0) for x in row_terms], [two], scaled)
    col_terms = [keep, got, ca_got, col_swap(to_x, x_=1), col_swap(to_l, l=1), col_swap(to_lx, l=1, x_=3)]
    return row_terms, col_terms


def row_sum(s):
    for kw in (dict(z=1), dict(z=3), dict(y=1), dict(y=3)):
        s = s + row_swap(s, **kw)
    return s


def prepare_kernel(row_ref, col_ref, count_ref, w_ref, wh, wl, th, tl, drow, dcol):
    step = pl.program_id(0)

    @pl.when(step == 0)
    def _():
        drow[...] = jnp.zeros_like(drow)
        dcol[...] = jnp.zeros_like(dcol)

    per = w_ref.shape[0]
    for j in range(per):
        k = step * per + j
        w = jnp.where(k < count_ref[0], w_ref[j], 0.0)
        t = w.T
        hi = w.astype(jnp.bfloat16)
        wh[j] = hi
        wl[j] = (w - hi.astype(jnp.float32)).astype(jnp.bfloat16)
        hi = t.astype(jnp.bfloat16)
        th[j] = hi
        tl[j] = (t - hi.astype(jnp.float32)).astype(jnp.bfloat16)
        first = lax.broadcasted_iota(jnp.int32, (8, BLK), 0) == 0
        r, c = row_ref[k], col_ref[k]
        drow[r] += jnp.where(first, jnp.sum(t, axis=0, keepdims=True), 0.0)
        dcol[c] += jnp.where(first, jnp.sum(w, axis=0, keepdims=True), 0.0)


def prepare(values, row_pos, col_pos, count):
    n = values.shape[0]
    per = 8
    nrow, ncol = 32, 32
    blk = pl.BlockSpec((per, BLK, BLK), lambda i, *_: (i, 0, 0))
    deg = pl.BlockSpec((nrow, 8, BLK), lambda i, *_: (0, 0, 0))
    half = jax.ShapeDtypeStruct((n, BLK, BLK), jnp.bfloat16)
    return pl.pallas_call(
        prepare_kernel,
        grid_spec=pltpu.PrefetchScalarGridSpec(
            num_scalar_prefetch=3, grid=(n // per,), in_specs=[blk], out_specs=[blk] * 4 + [deg] * 2
        ),
        out_shape=[half] * 4
        + [jax.ShapeDtypeStruct((nrow, 8, BLK), jnp.float32), jax.ShapeDtypeStruct((ncol, 8, BLK), jnp.float32)],
        compiler_params=pltpu.CompilerParams(vmem_limit_bytes=VMEM_LIMIT),
        name="prepare",
    )(row_pos, col_pos, count, values)


def product_kernel(n_in, unit, src_ref, dst_ref, *refs):
    refs = list(refs)
    wh, wl = refs[:2]
    xs = refs[2:2 + n_in]
    rest = refs[2 + n_in:]
    if unit > BLK:
        deg, rest = rest[0], rest[1:]
    outs, (xh, xl, acc) = rest[:-3], rest[-3:]
    if unit == BLK:
        top = jnp.zeros((8, BLK), jnp.float32)
        total = jnp.zeros((8, BLK), jnp.float32)
        for x in xs:
            size = jnp.abs(x[...]).reshape(-1, 8, BLK)
            top = jnp.maximum(top, jnp.max(size, axis=0))
            total += jnp.sum(size, axis=0)
        total = jnp.sum(total, axis=0, keepdims=True)
        top = jnp.max(top, axis=0, keepdims=True)
        scale = jnp.where(top > 1e-30, top, 1e-30)
    at = 0
    for x in xs:
        for b in range(x.shape[0] // BLK):
            v = x[b * BLK:(b + 1) * BLK, :]
            if unit == BLK:
                v = v / scale
            hi = v.astype(jnp.bfloat16)
            xh[at] = hi
            xl[at] = (v - hi.astype(jnp.float32)).astype(jnp.bfloat16)
            at += 1
    acc[...] = jnp.zeros_like(acc)
    group = 8

    @pl.loop(0, wh.shape[0] // group)
    def _(g):
        prods = []
        for j in range(group):
            k = g * group + j
            s = src_ref[k]
            a, b, c, d = wh[k], wl[k], xh[s], xl[s]
            p = jnp.dot(a, c, preferred_element_type=jnp.float32)
            p += jnp.dot(b, c, preferred_element_type=jnp.float32)
            p += jnp.dot(a, d, preferred_element_type=jnp.float32)
            prods.append(p)
        for j in range(group):
            d = dst_ref[g * group + j]
            acc[d] += prods[j]

    at = 0
    for o in outs:
        for b in range(o.shape[0] // unit):
            o[b * unit:b * unit + BLK, :] = acc[at]
            if unit > BLK:
                o[b * unit + BLK:(b + 1) * unit, :] = deg[at]
            at += 1
        if unit == BLK:
            o[o.shape[0] - 8:, :] = aux_tile(scale, total)


def product(src, dst, wh, wl, xs, sizes, deg=None):
    unit, tail = (BLK, 8) if deg is None else (BLK + 8, 0)
    smem = pl.BlockSpec(memory_space=pltpu.SMEM)
    vmem = pl.BlockSpec(memory_space=pltpu.VMEM)
    args = [wh, wl, *xs] + ([deg] if deg is not None else [])
    n = wh.shape[0]
    return pl.pallas_call(
        functools.partial(product_kernel, len(xs), unit),
        in_specs=[smem, smem] + [vmem] * len(args),
        out_specs=[vmem] * len(sizes),
        out_shape=[jax.ShapeDtypeStruct((s * unit + tail, BLK), jnp.float32) for s in sizes],
        scratch_shapes=[
            pltpu.VMEM((32, BLK, BLK), jnp.bfloat16),
            pltpu.VMEM((32, BLK, BLK), jnp.bfloat16),
            pltpu.VMEM((32, BLK, BLK), jnp.float32),
        ],
        compiler_params=pltpu.CompilerParams(vmem_limit_bytes=VMEM_LIMIT),
        cost_estimate=pl.CostEstimate(flops=6 * n * BLK**3, bytes_accessed=12 * 2**20, transcendentals=0),
        name="product",
    )(src, dst, *args)


def finish_first_kernel(*refs):
    terms, (y_ref, d_ref) = refs[:-2], refs[-2:]
    u = BLK + 8
    for b in range(2):
        t = weighted(terms, [0] * len(terms), [None] * len(terms), b * u, (b + 1) * u)
        d = jnp.broadcast_to(t[BLK:BLK + 1, :], (BLK, BLK)).T
        y_ref[b * BLK:(b + 1) * BLK, :] = t[:BLK] / d
        d_ref[b * BLK:(b + 1) * BLK, :] = d


def finish_kernel(docs, n_row, *refs):
    terms, (d_ref, y_ref, m_ref) = refs[:-3], refs[-3:]
    aux = [r[r.shape[0] - 8:, :] for r in terms]
    mean = functools.reduce(jnp.add, [a[1:2] for a in aux[:n_row]]) / docs
    weight = [a[:1] / mean for a in aux]
    y_ref[...] = weighted(terms, [0] * len(terms), weight, 0, 2 * BLK) / d_ref[...]
    m_ref[...] = jnp.broadcast_to(mean, (8, BLK))


def finish(row_terms, col_terms, deg, docs):
    vmem = pl.BlockSpec(memory_space=pltpu.VMEM)
    big = jax.ShapeDtypeStruct((2 * BLK, BLK), jnp.float32)
    if deg is None:
        kernel, extra, small = finish_first_kernel, [], big
    else:
        kernel, extra = functools.partial(finish_kernel, float(docs), len(row_terms)), [deg]
        small = jax.ShapeDtypeStruct((8, BLK), jnp.float32)
    args = [*row_terms, *col_terms, *extra]
    return pl.pallas_call(
        kernel,
        in_specs=[vmem] * len(args),
        out_specs=[vmem] * 2,
        out_shape=[big, small],
        compiler_params=pltpu.CompilerParams(vmem_limit_bytes=VMEM_LIMIT),
        name="finish",
    )(*args)


def position(order, index):
    order_pos = [order.index(m) for m in range(16)]
    out = jnp.zeros_like(index)
    for m in range(16):
        out = out + jnp.where(index == m, order_pos[m], 0)
    return out


def local(block_values, block_slot, block_count, probes):
    total_docs = probes.shape[0] * lax.axis_size("row") * lax.axis_size("col")
    slots = block_slot.reshape(-1)
    stored = slots.shape[0]
    local_row, local_col = slots // 32, slots % 32
    row_pos = 2 * position(COL_ORDER, (local_row // 2) ^ lax.axis_index("col")) + local_row % 2
    col_pos = 2 * position(ROW_ORDER, (local_col // 2) ^ lax.axis_index("row")) + local_col % 2
    wh, wl, th, tl, drow, dcol = prepare(
        block_values.reshape(stored, BLK, BLK), row_pos, col_pos, block_count.reshape(1)
    )
    y, deg, mean = probes, None, None
    for t in range(ITERS):
        first = t == 0
        before = y
        rows, cols = gather(y, (wh,) if first else ())
        back = product(row_pos, col_pos, th, tl, cols, [8] * 4, dcol if first else None)
        fwd = product(col_pos, row_pos, wh, wl, rows, [16, 16], drow if first else None)
        terms = scatter(back, fwd, BLK + (8 if first else 0), not first)
        if first:
            y, deg = finish(*terms, None, total_docs)
        else:
            y, mean = finish(*terms, deg, total_docs)
    part = jnp.sum(jnp.abs(y).reshape(-1, 8, BLK), axis=0)
    part = jnp.sum(lax.all_to_all(jnp.broadcast_to(part, (16, 8, BLK)), "col", 0, 0, tiled=True), axis=0)
    final = jnp.sum(row_sum(part), axis=0, keepdims=True) / total_docs
    embedding = y / final
    return embedding, embedding - before / mean[:1]


def solution(mesh):
    in_specs = (
        P("row", "col", None, None, None),
        P("row", "col", None),
        P("row", "col"),
        P(("row", "col"), None),
    )
    out_specs = (P(("row", "col"), None), P(("row", "col"), None))
    return jax.shard_map(local, mesh=mesh, in_specs=in_specs, out_specs=out_specs, check_vma=False)
```
